256 devices in a mesh: grp: 8 (over x_hi, y), mem: 32 (over z, x_lo, core).
Axes of the slice: x: 4 (x_hi: 2, x_lo: 2; x = x_hi * 2 + x_lo), y: 4, z: 8, core: 2. Of those that a mesh axis runs over, the one named last changes fastest.
Arguments:
- contracted_amplitudes: bfloat16 [1024, 32768], P('mem', 'grp'), may hold values from -6 to 6
- ladder_integrals: bfloat16 [32768, 32768], P('grp', 'mem'), may hold values from -0.046875 to 0.046875
- cd_pairs: int32 [8, 2], P('grp'), may hold values from 0 to 18, as said below
- block_irrep: int32 [19], replicated, may hold values from 0 to 7, as said below
- ab_blocks: int32 [8, 2], replicated, may hold values from 0 to 18, as said below
- amps_ab: bfloat16 [1024, 32768], P(('grp', 'mem')), may hold values from -6 to 6
- dressing: bfloat16 [19, 64, 64], replicated, may hold values from -0.75 to 0.75
- occ_energy: float32 [120], replicated, may hold values from -2 to -0.3
- virt_energy: float32 [1216], replicated, may hold values from 0.5 to 3
- pair_occ: int32 [1024, 2], P(('grp', 'mem')), may hold values from 0 to 119
Outputs:
- new_amps: float32 [1024, 32768], P(('grp', 'mem'))
The draws below stay inside these ranges and needn't reach their ends.
Inputs may be any that keep to these rules, and one draw needn't show every extreme that they name: Every row of ab_blocks names two blocks whose irreps XOR to the same symmetry. `cd_pairs`: each index of grp holds 1 row; some index of grp holds a row with the symmetry of ab_blocks, and some other index holds none. `block_irrep`: every irrep 0 to 7 labels at least one block.
All inputs are finite; a program needn't handle non-finite values.
Results may differ from the reference program's by a relative error of at most 0.0003.
Values may be sent and summed in bfloat16 or wider, within the bound.
No kernel may reach another device: no remote copies, remote signals or barrier semaphores. Data moves between devices by JAX's collectives and lax.ppermute only.
A program may use at most 64 MiB of HBM per device.

```python
import jax
import jax.numpy as jnp
from jax import lax

BV = 64
NB = 19
NOCC = 120
SLOTS = 1
SLAB_PAIRS = 1024
VIRTUAL_PAIRS = 4096
OUTPUT_PAIRS = 8
CONTRACTED_PAIRS = 8
N_GRP = 8


def orbital_labels(key):
    extra = jax.random.randint(jax.random.fold_in(key, 101), (NB - 8,), 0, 8)
    labels = jnp.concatenate([jnp.arange(8, dtype=jnp.int32), extra.astype(jnp.int32)])
    labels = jax.random.permutation(jax.random.fold_in(key, 102), labels)
    target = jax.random.randint(jax.random.fold_in(key, 103), (), 0, 8).astype(jnp.int32)
    return (labels.astype(jnp.int32), target)


def pick_block(key, labels, wanted):
    scores = jax.random.randint(key, wanted.shape + (NB,), 0, 1 << 20) * NB + jnp.arange(NB, dtype=jnp.int32)
    scores = jnp.where(labels == wanted[..., None], scores, -1)
    return lax.top_k(scores, 1)[1][..., 0].astype(jnp.int32)


def draw_block_irrep(key, part):
    labels, target = orbital_labels(key)
    return labels


def draw_ab_blocks(key, part):
    labels, target = orbital_labels(key)
    key = jax.random.fold_in(key, 11)
    first = jax.random.randint(jax.random.fold_in(key, 1), (OUTPUT_PAIRS,), 0, NB).astype(jnp.int32)
    first = first.at[0].set(0).at[OUTPUT_PAIRS - 1].set(NB - 1)
    wanted = jnp.bitwise_xor(labels[first], target)
    second = pick_block(jax.random.fold_in(key, 2), labels, wanted)
    return jnp.stack([first, second], axis=-1)


def draw_cd_pairs(key, part):
    labels, target = orbital_labels(key)
    key = jax.random.fold_in(key, 12)
    first = jax.random.randint(jax.random.fold_in(key, 1), (N_GRP * SLOTS,), 0, NB).astype(jnp.int32)
    first = first.at[0].set(0).at[N_GRP * SLOTS - 1].set(NB - 1).reshape(N_GRP, SLOTS)
    coin = jax.random.randint(jax.random.fold_in(key, 2), (N_GRP, SLOTS), 0, 2) == 1
    full_group = jax.random.randint(jax.random.fold_in(key, 3), (), 0, N_GRP)
    dead_group = (full_group + jax.random.randint(jax.random.fold_in(key, 4), (), 1, N_GRP)) % N_GRP
    group_ids = jnp.arange(N_GRP)[:, None]
    allowed = jnp.where(group_ids == full_group, True, jnp.where(group_ids == dead_group, False, coin))
    flip = jax.random.randint(jax.random.fold_in(key, 5), (N_GRP, SLOTS), 1, 8)
    wanted = jnp.bitwise_xor(jnp.bitwise_xor(labels[first], target), jnp.where(allowed, 0, flip)).astype(jnp.int32)
    second = pick_block(jax.random.fold_in(key, 6), labels, wanted)
    return jnp.stack([first, second], axis=-1).reshape(N_GRP * SLOTS, 2)


def set_ends(array, stream_key, smallest, high):
    place = [jax.random.randint(jax.random.fold_in(stream_key, axis), (), 0, length) for axis, length in enumerate(array.shape)]
    longest = array.shape.index(max(array.shape))
    beside = place[:longest] + [(place[longest] + 1) % array.shape[longest]] + place[longest + 1:]
    return array.at[tuple(place)].set(smallest).at[tuple(beside)].set(high)


def block_scale(own_key, extent, pieces, least, largest):
    def one(dim, blocks):
        steps = jax.random.uniform(jax.random.fold_in(jax.random.fold_in(own_key, 6), dim), (blocks,), jnp.float32, least / len(pieces), largest / len(pieces))
        return jnp.repeat(jnp.exp(steps), extent[dim] // blocks).reshape((-1,) + (1,) * (len(extent) - dim - 1))

    factor_of = one(*pieces[0])
    for cut in pieces[1:]:
        factor_of = factor_of * one(*cut)
    return factor_of


def scatter_about(rng, shape, scale, reach, pieces=(), held_as=jnp.bfloat16):
    loudness = block_scale(rng, shape, pieces, -0.22, 0.18) if pieces else 1.0
    drawn = jax.random.normal(rng, shape, jnp.float32) * scale * loudness
    return jnp.minimum(jnp.maximum(drawn, -reach), reach).astype(held_as)


def setup_inputs(seed: int = 0) -> dict:
    keys = jax.random.split(jax.random.key(seed), 11)
    return {
        "contracted_amplitudes": scatter_about(keys[0], (SLAB_PAIRS, CONTRACTED_PAIRS * VIRTUAL_PAIRS), 1.0, 6.0, ((0, 32), (1, 8))),
        "ladder_integrals": scatter_about(keys[1], (CONTRACTED_PAIRS * VIRTUAL_PAIRS, OUTPUT_PAIRS * VIRTUAL_PAIRS), (CONTRACTED_PAIRS * VIRTUAL_PAIRS // 2) ** -0.5, 0.046875, ((0, 8), (1, 32))),
        "cd_pairs": draw_cd_pairs(jax.random.fold_in(keys[10], 71), 0),
        "block_irrep": draw_block_irrep(jax.random.fold_in(keys[10], 71), 0),
        "ab_blocks": draw_ab_blocks(jax.random.fold_in(keys[10], 71), 0),
        "amps_ab": scatter_about(keys[5], (SLAB_PAIRS, OUTPUT_PAIRS * VIRTUAL_PAIRS), 1.0, 6.0, ((0, 256),)),
        "dressing": scatter_about(keys[6], (NB, BV, BV), BV ** -0.5, 0.75),
        "occ_energy": jnp.clip(jax.random.uniform(keys[7], (NOCC,), jnp.float32, -2.0, -0.3), -2.0, -0.3),
        "virt_energy": jnp.clip(jax.random.uniform(keys[8], (NB * BV,), jnp.float32, 0.5, 3.0), 0.5, 3.0),
        "pair_occ": set_ends(jax.random.randint(keys[9], (SLAB_PAIRS, 2), 0, NOCC), jax.random.fold_in(keys[9], 1), 0, NOCC - 1).astype(jnp.int32),
    }


def reference(contracted_amplitudes, ladder_integrals, cd_pairs, block_irrep, ab_blocks, amps_ab, dressing, occ_energy, virt_energy, pair_occ):
    target = jnp.bitwise_xor(block_irrep[ab_blocks[0, 0]], block_irrep[ab_blocks[0, 1]])
    symmetry = jnp.bitwise_xor(block_irrep[cd_pairs[:, 0]], block_irrep[cd_pairs[:, 1]])
    allowed = (symmetry == target).astype(jnp.float32)
    ladder = jnp.zeros((SLAB_PAIRS, OUTPUT_PAIRS * VIRTUAL_PAIRS), jnp.float32)
    for contracted_slot_index in range(CONTRACTED_PAIRS):
        amp_slot = contracted_amplitudes[:, contracted_slot_index * VIRTUAL_PAIRS:(contracted_slot_index + 1) * VIRTUAL_PAIRS]
        int_slot = ladder_integrals[contracted_slot_index * VIRTUAL_PAIRS:(contracted_slot_index + 1) * VIRTUAL_PAIRS, :]
        ladder = ladder + allowed[contracted_slot_index] * jnp.dot(amp_slot, int_slot, preferred_element_type=jnp.float32)
    amp_blocks = amps_ab.astype(jnp.float32).reshape(SLAB_PAIRS, OUTPUT_PAIRS, BV, BV)
    left_dress = dressing[ab_blocks[:, 0]].astype(jnp.float32)
    right_dress = dressing[ab_blocks[:, 1]].astype(jnp.float32)
    dressed = jnp.einsum('nac,pncb->pnab', left_dress, amp_blocks, precision=lax.Precision.HIGHEST)
    dressed = dressed + jnp.einsum('nbc,pnac->pnab', right_dress, amp_blocks, precision=lax.Precision.HIGHEST)
    virt_blocks = virt_energy.reshape(NB, BV)
    left_energy = virt_blocks[ab_blocks[:, 0]]
    right_energy = virt_blocks[ab_blocks[:, 1]]
    occ_sum = occ_energy[pair_occ[:, 0]] + occ_energy[pair_occ[:, 1]]
    denominator = (left_energy[None, :, :, None] + right_energy[None, :, None, :]) - occ_sum[:, None, None, None]
    result = (ladder.reshape(SLAB_PAIRS, OUTPUT_PAIRS, BV, BV) + dressed) / denominator
    return result.reshape(SLAB_PAIRS, OUTPUT_PAIRS * VIRTUAL_PAIRS)
```

```python
import jax
import jax.numpy as jnp
from jax import lax
from jax.sharding import PartitionSpec as P

Z = 8
MEM = 32


def pairs(target):
    return [(i, target(i)) for i in range(MEM)]


RING = pairs(lambda i: (i + 4) % MEM if i % 2 == 0 else (i - 4) % MEM)
NEIGHBOUR = pairs(lambda i: i ^ 2)
SIBLING = pairs(lambda i: i ^ 1)


def send(x, perm):
    return lax.ppermute(x, "mem", perm)


def stack(*blocks):
    return jnp.concatenate(blocks, axis=0)


def gathered_slots(own):
    a = [own, send(own, RING)]
    b0 = send(own, SIBLING)
    x0 = send(own, NEIGHBOUR)
    b = [b0, send(b0, RING)]
    a.append(send(a[1], RING))
    q = [x0, send(x0, RING)]
    bx = send(x0, SIBLING)
    r = [None]
    for k in (1, 2):
        b.append(send(b[k], RING))
        r.append(send(b[k], NEIGHBOUR))
        a.append(send(a[k + 1], RING))
        q.append(send(q[k], RING))
    r.append(send(b[3], NEIGHBOUR))
    q.append(send(q[3], RING))
    out = [((0,), stack(own, b0, x0, bx))]
    for k in (1, 2, 3):
        other = send(stack(b[k], a[k], r[k], q[k]), SIBLING)
        out.append(((k, Z - k), stack(a[k], b[k], q[k], r[k], other)))
    other = send(stack(a[4], q[4]), SIBLING)
    rows = own.shape[0]
    out.append(((4,), stack(a[4], other[:rows], q[4], other[rows:])))
    return out


def local(
    contracted_amplitudes,
    ladder_integrals,
    cd_pairs,
    block_irrep,
    ab_blocks,
    amps_ab,
    dressing,
    occ_energy,
    virt_energy,
    pair_occ,
):
    shard_rows = contracted_amplitudes.shape[0]
    col_count = ladder_integrals.shape[1]
    local_rows = amps_ab.shape[0]
    slot_rows = 4 * shard_rows
    block_width = dressing.shape[1]
    pair_width = block_width * block_width
    block_total = dressing.shape[0]
    block_ids = jnp.arange(block_total, dtype=jnp.int32)
    pair_onehot = (cd_pairs[:, :, None] == block_ids[None, None, :]).astype(jnp.int32)
    pair_irreps = jnp.sum(pair_onehot * block_irrep[None, None, :], axis=-1)
    out_onehot = (ab_blocks[:, :, None] == block_ids[None, None, :]).astype(jnp.int32)
    out_irreps = jnp.sum(out_onehot * block_irrep[None, None, :], axis=-1)
    target = jnp.bitwise_xor(out_irreps[0, 0], out_irreps[0, 1])
    allowed = jnp.bitwise_xor(pair_irreps[0, 0], pair_irreps[0, 1]) == target
    scale = allowed.astype(jnp.float32) * 32.0

    member = lax.axis_index("mem")
    z = member // 4
    x_lo = (member // 2) % 2
    core = member % 2
    sign = 2 * core - 1

    partial = jnp.zeros((Z, slot_rows, col_count), jnp.float16)
    for slots, rows in gathered_slots(contracted_amplitudes):
        product = jnp.dot(rows, ladder_integrals, preferred_element_type=jnp.float32)
        product = (product * scale).astype(jnp.float16)
        for n, slot in enumerate(slots):
            owner = jnp.mod(z + sign * slot, Z)
            part = product[n * slot_rows : (n + 1) * slot_rows]
            partial = lax.dynamic_update_slice(partial, part[None], (owner, 0, 0))
    summed = jnp.sum(
        lax.all_to_all(partial, "grp", split_axis=0, concat_axis=0).astype(jnp.float32), axis=0
    ) * (1.0 / 32.0)
    summed = summed.reshape(2, 2, shard_rows, col_count)
    summed = jnp.where(x_lo == 1, summed[::-1], summed)
    summed = jnp.where(core == 1, summed[:, ::-1], summed)
    summed = summed.reshape(MEM, local_rows, col_count)
    ladder = lax.all_to_all(summed, "mem", split_axis=0, concat_axis=0)

    out_pairs = ab_blocks.shape[0]
    left_select = out_onehot[:, 0, :].astype(jnp.float32)
    right_select = out_onehot[:, 1, :].astype(jnp.float32)
    dress_flat = dressing.reshape(block_total, pair_width).astype(jnp.float32)
    left_dress = jnp.dot(left_select, dress_flat, precision=lax.Precision.HIGHEST).reshape(
        out_pairs, block_width, block_width
    )
    right_dress = jnp.dot(right_select, dress_flat, precision=lax.Precision.HIGHEST).reshape(
        out_pairs, block_width, block_width
    )
    amp_blocks = amps_ab.astype(jnp.float32).reshape(
        local_rows, out_pairs, block_width, block_width
    )
    dressed = jnp.einsum("nac,pncb->pnab", left_dress, amp_blocks, precision=lax.Precision.HIGHEST)
    dressed = dressed + jnp.einsum(
        "nbc,pnac->pnab", right_dress, amp_blocks, precision=lax.Precision.HIGHEST
    )
    virt_blocks = virt_energy.reshape(block_total, block_width)
    left_energy = jnp.dot(left_select, virt_blocks, precision=lax.Precision.HIGHEST)
    right_energy = jnp.dot(right_select, virt_blocks, precision=lax.Precision.HIGHEST)
    occ_ids = jnp.arange(occ_energy.shape[0], dtype=jnp.int32)
    occ_onehot = (pair_occ[:, :, None] == occ_ids[None, None, :]).astype(jnp.float32)
    occ_pick = jnp.sum(occ_onehot * occ_energy[None, None, :], axis=-1)
    occ_sum = occ_pick[:, 0] + occ_pick[:, 1]
    denominator = (
        left_energy[None, :, :, None]
        + right_energy[None, :, None, :]
        - occ_sum[:, None, None, None]
    )
    width = out_pairs * pair_width
    dressed = dressed.reshape(local_rows, width)
    denominator = denominator.reshape(local_rows, width)
    ladder = ladder.transpose(1, 0, 2).reshape(local_rows, width)
    return (ladder + dressed) / denominator


def solution(mesh):
    return jax.shard_map(
        local,
        mesh=mesh,
        in_specs=(
            P("mem", "grp"),
            P("grp", "mem"),
            P("grp", None),
            P(),
            P(),
            P(("grp", "mem"), None),
            P(),
            P(),
            P(),
            P(("grp", "mem"), None),
        ),
        out_specs=P(("grp", "mem"), None),
        check_vma=False,
    )
```

```python
import jax
import jax.numpy as jnp
from jax import lax
from jax.experimental import pallas as pl
from jax.experimental.pallas import tpu as pltpu
from jax.sharding import PartitionSpec as P

Z = 8
MEM = 32


def pairs(target):
    return [(i, target(i)) for i in range(MEM)]


RING = pairs(lambda i: (i + 4) % MEM if i % 2 == 0 else (i - 4) % MEM)
NEIGHBOUR = pairs(lambda i: i ^ 2)
SIBLING = pairs(lambda i: i ^ 1)
RING_SIBLING = pairs(lambda i: (i - 3) % MEM if i % 2 == 0 else (i + 3) % MEM)
RING_NEIGHBOUR = pairs(lambda i: ((i + 4) % MEM if i % 2 == 0 else (i - 4) % MEM) ^ 2)


SLOTS = (0, 1, Z - 1, 2, Z - 2, 3, Z - 3, 4)
OWNERS = [[(i // 4 + (2 * (i % 2) - 1) * s) % Z * MEM + i for s in SLOTS] for i in range(MEM)]


def send(x, perm):
    return lax.ppermute(x, "mem", perm)


def stack(*blocks):
    return jnp.concatenate(blocks, axis=0)


def after(x, *done):
    return lax.optimization_barrier((x, *done))[0]


def ladder_partial(own, ready, multiply):
    rows = own.shape[0]
    a1 = send(own, RING)
    b1 = send(own, RING_SIBLING)
    q1 = send(own, RING_NEIGHBOUR)
    b0 = send(own, SIBLING)
    x0 = send(own, NEIGHBOUR)

    a1 = after(a1, ready)
    a2 = send(a1, RING)
    b1 = after(b1, a1)
    r1 = send(b1, NEIGHBOUR)
    b2 = send(b1, RING)
    q1 = after(q1, b1)
    q2 = send(q1, RING)

    a2 = after(a2, q1)
    a3 = send(a2, RING)
    b2 = after(b2, a2)
    b3 = send(b2, RING)
    r2 = send(b2, NEIGHBOUR)
    q2 = after(q2, b2)
    q3 = send(q2, RING)
    x0 = after(x0, q2)
    bx = send(x0, SIBLING)

    a3 = after(a3, x0)
    a4 = send(a3, RING)
    r1 = after(r1, a3)
    c1 = send(stack(b1, a1, r1, q1), SIBLING)
    b3 = after(b3, r1)
    r3 = send(b3, NEIGHBOUR)
    q3 = after(q3, b3)
    q4 = send(q3, RING)
    r2 = after(r2, q3)
    c2 = send(stack(b2, a2, r2, q2), SIBLING)
    product = multiply(stack(after(own, r2), b0, x0, bx, a1, b1, q1, r1, c1))
    partial = jnp.pad(product, ((0, 20 * rows), (0, 0)))

    c2 = after(c2, partial)
    product = multiply(stack(a2, b2, q2, r2, c2))
    partial = lax.dynamic_update_slice(partial, product, (12 * rows, 0))
    a4 = after(a4, partial)
    r3 = after(r3, a4)
    c3 = send(stack(b3, a3, r3, q3), SIBLING)
    q4 = after(q4, r3)
    c4 = send(stack(a4, q4), SIBLING)
    product = multiply(stack(a3, b3, q3, r3, c3, a4, c4[:rows], q4, c4[rows:]))
    return lax.dynamic_update_slice(partial, product, (20 * rows, 0))


def mask_kernel(cd_pairs, block_irrep, ab_blocks, scale):
    target = block_irrep[ab_blocks[0, 0]] ^ block_irrep[ab_blocks[1, 0]]
    symmetry = block_irrep[cd_pairs[0, 0]] ^ block_irrep[cd_pairs[0, 1]]
    scale[...] = jnp.full(scale.shape, jnp.where(symmetry == target, 32.0, 0.0), jnp.float32)


def local(
    contracted_amplitudes,
    ladder_integrals,
    cd_pairs,
    block_irrep,
    ab_blocks,
    amps_ab,
    dressing,
    occ_energy,
    virt_energy,
    pair_occ,
):
    col_count = ladder_integrals.shape[1]
    local_rows = amps_ab.shape[0]
    block_width = dressing.shape[1]
    pair_width = block_width * block_width
    block_total = dressing.shape[0]
    block_ids = jnp.arange(block_total, dtype=jnp.int32)
    out_onehot = (ab_blocks[:, :, None] == block_ids[None, None, :]).astype(jnp.int32)
    scale = pl.pallas_call(
        mask_kernel,
        out_shape=jax.ShapeDtypeStruct((1, 128), jnp.float32),
        in_specs=[pl.BlockSpec(memory_space=pltpu.SMEM)] * 3,
        out_specs=pl.BlockSpec(memory_space=pltpu.VMEM),
        compiler_params=pltpu.CompilerParams(vmem_limit_bytes=1 << 20),
    )(cd_pairs, block_irrep, ab_blocks.T)

    member = lax.axis_index("mem")
    x_lo = (member // 2) % 2
    core = member % 2

    def multiply(rows):
        rows = lax.optimization_barrier(rows)
        product = jnp.dot(rows, ladder_integrals, preferred_element_type=jnp.float32)
        return (product * scale[0, 0]).astype(jnp.float16)

    partial = ladder_partial(contracted_amplitudes, scale, multiply)
    partial = partial.reshape(Z, -1, col_count)
    partial = lax.all_to_all(partial, ("grp", "mem"), split_axis=0, concat_axis=0, axis_index_groups=OWNERS)
    summed = jnp.sum(partial.astype(jnp.float32), axis=0) * (1.0 / 32.0)
    summed = summed.reshape(2, 2, -1, col_count)
    summed = jnp.where(x_lo == 1, summed[::-1], summed)
    summed = jnp.where(core == 1, summed[:, ::-1], summed)
    lanes = col_count // 8
    summed = summed.reshape(MEM, local_rows, -1, lanes).transpose(0, 2, 1, 3).reshape(MEM, -1, lanes)
    depth = summed.shape[1]
    place = jnp.arange(depth, dtype=jnp.float32)[None, :, None]
    largest = jnp.maximum(jnp.max(jnp.abs(summed), axis=1, keepdims=True), 1e-30)
    step = jnp.ceil(jnp.log2(largest * (1.0 / 16300.0)) * 256.0)
    shifted = (step + 32768.0) * jnp.exp2(-place)
    bits = jnp.floor(shifted) - 2.0 * jnp.floor(shifted * 0.5)
    coded = 2.0 * jnp.round(summed * jnp.exp2(step * (-1.0 / 256.0))) + bits
    coded = lax.all_to_all(coded.astype(jnp.int16), "mem", split_axis=0, concat_axis=0).astype(jnp.float32)
    code = jnp.floor(coded * 0.5)
    weight = jnp.where(place < 16.0, jnp.exp2(place), 0.0)
    step = jnp.sum((coded - 2.0 * code) * weight, axis=1, keepdims=True) - 32768.0
    ladder = code * jnp.exp2(step * (1.0 / 256.0))
    ladder = ladder.reshape(MEM, -1, local_rows, lanes).transpose(0, 2, 1, 3).reshape(MEM, local_rows, col_count)

    out_pairs = ab_blocks.shape[0]
    left_select = out_onehot[:, 0, :].astype(jnp.float32)
    right_select = out_onehot[:, 1, :].astype(jnp.float32)
    dress_flat = dressing.reshape(block_total, pair_width).astype(jnp.float32)
    left_dress = jnp.dot(left_select, dress_flat, precision=lax.Precision.HIGHEST).reshape(
        out_pairs, block_width, block_width
    )
    right_dress = jnp.dot(right_select, dress_flat, precision=lax.Precision.HIGHEST).reshape(
        out_pairs, block_width, block_width
    )
    amp_blocks = amps_ab.astype(jnp.float32).reshape(
        local_rows, out_pairs, block_width, block_width
    )
    dressed = jnp.einsum("nac,pncb->pnab", left_dress, amp_blocks, precision=lax.Precision.HIGHEST)
    dressed = dressed + jnp.einsum(
        "nbc,pnac->pnab", right_dress, amp_blocks, precision=lax.Precision.HIGHEST
    )
    virt_blocks = virt_energy.reshape(block_total, block_width)
    left_energy = jnp.dot(left_select, virt_blocks, precision=lax.Precision.HIGHEST)
    right_energy = jnp.dot(right_select, virt_blocks, precision=lax.Precision.HIGHEST)
    occ_ids = jnp.arange(occ_energy.shape[0], dtype=jnp.int32)
    occ_onehot = (pair_occ[:, :, None] == occ_ids[None, None, :]).astype(jnp.float32)
    occ_pick = jnp.sum(occ_onehot * occ_energy[None, None, :], axis=-1)
    occ_sum = occ_pick[:, 0] + occ_pick[:, 1]
    denominator = (
        left_energy[None, :, :, None]
        + right_energy[None, :, None, :]
        - occ_sum[:, None, None, None]
    )
    width = out_pairs * pair_width
    dressed = dressed.reshape(local_rows, width)
    denominator = denominator.reshape(local_rows, width)
    ladder = ladder.transpose(1, 0, 2).reshape(local_rows, width)
    return (ladder + dressed) / denominator


def solution(mesh):
    return jax.shard_map(
        local,
        mesh=mesh,
        in_specs=(
            P("mem", "grp"),
            P("grp", "mem"),
            P("grp", None),
            P(),
            P(),
            P(("grp", "mem"), None),
            P(),
            P(),
            P(),
            P(("grp", "mem"), None),
        ),
        out_specs=P(("grp", "mem"), None),
        check_vma=False,
    )
```

```python
import jax
import jax.numpy as jnp
from jax import lax
from jax.experimental import pallas as pl
from jax.experimental.pallas import tpu as pltpu
from jax.sharding import PartitionSpec as P

Z = 8
MEM = 32


def pairs(target):
    return [(i, target(i)) for i in range(MEM)]


RING = pairs(lambda i: (i + 4) % MEM if i % 2 == 0 else (i - 4) % MEM)
NEIGHBOUR = pairs(lambda i: i ^ 2)
SIBLING = pairs(lambda i: i ^ 1)
RING_SIBLING = pairs(lambda i: (i - 3) % MEM if i % 2 == 0 else (i + 3) % MEM)
RING_NEIGHBOUR = pairs(lambda i: ((i + 4) % MEM if i % 2 == 0 else (i - 4) % MEM) ^ 2)


SLOTS = (0, 1, Z - 1, 2, Z - 2, 3, Z - 3, 4)
OWNERS = [[(i // 4 + (2 * (i % 2) - 1) * s) % Z * MEM + i for s in SLOTS] for i in range(MEM)]


def send(x, perm):
    return lax.ppermute(x, "mem", perm)


def stack(*blocks):
    return jnp.concatenate(blocks, axis=0)


def after(x, *done):
    return lax.optimization_barrier((x, *done))[0]


def ladder_partial(own, ready, multiply):
    rows = own.shape[0]
    a1 = send(own, RING)
    b1 = send(own, RING_SIBLING)
    q1 = send(own, RING_NEIGHBOUR)
    b0 = send(own, SIBLING)
    x0 = send(own, NEIGHBOUR)

    a1 = after(a1, ready)
    a2 = send(a1, RING)
    b1 = after(b1, a1, b0)
    b2 = send(b1, RING)
    r1 = send(b1, NEIGHBOUR)
    q1 = after(q1, b1)
    q2 = send(q1, RING)
    x0 = after(x0, q1)
    bx = send(x0, SIBLING)

    a2 = after(a2, x0)
    a3 = send(a2, RING)
    b2 = after(b2, a2, bx)
    b3 = send(b2, RING)
    r2 = send(b2, NEIGHBOUR)
    q2 = after(q2, b2)
    q3 = send(q2, RING)
    r1 = after(r1, q2)
    near = stack(b1, a1, r1, q1)
    c1 = send(near, SIBLING)

    a3 = after(a3, near)
    a4 = send(a3, RING)
    b3 = after(b3, a3, c1)
    r3 = send(b3, NEIGHBOUR)
    q3 = after(q3, b3)
    q4 = send(q3, RING)
    r2 = after(r2, q3)
    middle = stack(b2, a2, r2, q2)
    c2 = send(middle, SIBLING)
    product = multiply(stack(after(own, middle), b0, x0, bx, a1, b1, q1, r1, c1))
    partial = jnp.pad(product, ((0, 20 * rows), (0, 0)))

    c2 = after(c2, partial)
    product = multiply(stack(a2, b2, q2, r2, c2))
    partial = lax.dynamic_update_slice(partial, product, (12 * rows, 0))
    a4 = after(a4, partial)
    r3 = after(r3, a4)
    c3 = send(stack(b3, a3, r3, q3), SIBLING)
    q4 = after(q4, r3)
    c4 = send(stack(a4, q4), SIBLING)
    product = multiply(stack(a3, b3, q3, r3, c3, a4, c4[:rows], q4, c4[rows:]))
    return lax.dynamic_update_slice(partial, product, (20 * rows, 0))


def mask_kernel(cd_pairs, block_irrep, ab_blocks, scale):
    target = block_irrep[ab_blocks[0, 0]] ^ block_irrep[ab_blocks[1, 0]]
    symmetry = block_irrep[cd_pairs[0, 0]] ^ block_irrep[cd_pairs[0, 1]]
    scale[...] = jnp.full(scale.shape, jnp.where(symmetry == target, 32.0, 0.0), jnp.float32)


def local(
    contracted_amplitudes,
    ladder_integrals,
    cd_pairs,
    block_irrep,
    ab_blocks,
    amps_ab,
    dressing,
    occ_energy,
    virt_energy,
    pair_occ,
):
    col_count = ladder_integrals.shape[1]
    local_rows = amps_ab.shape[0]
    block_width = dressing.shape[1]
    pair_width = block_width * block_width
    block_total = dressing.shape[0]
    block_ids = jnp.arange(block_total, dtype=jnp.int32)
    out_onehot = (ab_blocks[:, :, None] == block_ids[None, None, :]).astype(jnp.int32)
    scale = pl.pallas_call(
        mask_kernel,
        out_shape=jax.ShapeDtypeStruct((1, 128), jnp.float32),
        in_specs=[pl.BlockSpec(memory_space=pltpu.SMEM)] * 3,
        out_specs=pl.BlockSpec(memory_space=pltpu.VMEM),
        compiler_params=pltpu.CompilerParams(vmem_limit_bytes=1 << 20),
    )(cd_pairs, block_irrep, ab_blocks.T)

    member = lax.axis_index("mem")
    x_lo = (member // 2) % 2
    core = member % 2

    def multiply(rows):
        rows = lax.optimization_barrier(rows)
        product = jnp.dot(rows, ladder_integrals, preferred_element_type=jnp.float32)
        return (product * scale[0, 0]).astype(jnp.float16)

    partial = ladder_partial(contracted_amplitudes, scale, multiply)
    partial = partial.reshape(Z, -1, col_count)
    partial = lax.all_to_all(partial, ("grp", "mem"), split_axis=0, concat_axis=0, axis_index_groups=OWNERS)
    summed = jnp.sum(partial.astype(jnp.float32), axis=0)
    summed = summed.reshape(2, 2, -1, col_count)
    summed = jnp.where(x_lo == 1, summed[::-1], summed)
    summed = jnp.where(core == 1, summed[:, ::-1], summed)
    summed = summed.reshape(MEM, local_rows, col_count).astype(jnp.float16)
    ladder = lax.all_to_all(summed, "mem", split_axis=0, concat_axis=0).astype(jnp.float32) * (1.0 / 32.0)

    out_pairs = ab_blocks.shape[0]
    left_select = out_onehot[:, 0, :].astype(jnp.float32)
    right_select = out_onehot[:, 1, :].astype(jnp.float32)
    dress_flat = dressing.reshape(block_total, pair_width).astype(jnp.float32)
    left_dress = jnp.dot(left_select, dress_flat, precision=lax.Precision.HIGHEST).reshape(
        out_pairs, block_width, block_width
    )
    right_dress = jnp.dot(right_select, dress_flat, precision=lax.Precision.HIGHEST).reshape(
        out_pairs, block_width, block_width
    )
    amp_blocks = amps_ab.astype(jnp.float32).reshape(
        local_rows, out_pairs, block_width, block_width
    )
    dressed = jnp.einsum("nac,pncb->pnab", left_dress, amp_blocks, precision=lax.Precision.HIGHEST)
    dressed = dressed + jnp.einsum(
        "nbc,pnac->pnab", right_dress, amp_blocks, precision=lax.Precision.HIGHEST
    )
    virt_blocks = virt_energy.reshape(block_total, block_width)
    left_energy = jnp.dot(left_select, virt_blocks, precision=lax.Precision.HIGHEST)
    right_energy = jnp.dot(right_select, virt_blocks, precision=lax.Precision.HIGHEST)
    occ_ids = jnp.arange(occ_energy.shape[0], dtype=jnp.int32)
    occ_onehot = (pair_occ[:, :, None] == occ_ids[None, None, :]).astype(jnp.float32)
    occ_pick = jnp.sum(occ_onehot * occ_energy[None, None, :], axis=-1)
    occ_sum = occ_pick[:, 0] + occ_pick[:, 1]
    denominator = (
        left_energy[None, :, :, None]
        + right_energy[None, :, None, :]
        - occ_sum[:, None, None, None]
    )
    width = out_pairs * pair_width
    dressed = dressed.reshape(local_rows, width)
    denominator = denominator.reshape(local_rows, width)
    ladder = ladder.transpose(1, 0, 2).reshape(local_rows, width)
    return (ladder + dressed) / denominator


def solution(mesh):
    return jax.shard_map(
        local,
        mesh=mesh,
        in_specs=(
            P("mem", "grp"),
            P("grp", "mem"),
            P("grp", None),
            P(),
            P(),
            P(("grp", "mem"), None),
            P(),
            P(),
            P(),
            P(("grp", "mem"), None),
        ),
        out_specs=P(("grp", "mem"), None),
        check_vma=False,
    )
```

```python
import jax
import jax.numpy as jnp
from jax import lax
from jax.experimental import pallas as pl
from jax.experimental.pallas import tpu as pltpu
from jax.sharding import PartitionSpec as P

Z = 8
MEM = 32


def pairs(target):
    return [(i, target(i)) for i in range(MEM)]


RING = pairs(lambda i: (i + 4) % MEM if i % 2 == 0 else (i - 4) % MEM)
NEIGHBOUR = pairs(lambda i: i ^ 2)
SIBLING = pairs(lambda i: i ^ 1)
RING_SIBLING = pairs(lambda i: (i - 3) % MEM if i % 2 == 0 else (i + 3) % MEM)
RING_NEIGHBOUR = pairs(lambda i: ((i + 4) % MEM if i % 2 == 0 else (i - 4) % MEM) ^ 2)


SLOTS = (0, 1, Z - 1, 2, Z - 2, 3, Z - 3, 4)
OWNERS = [[(i // 4 + (2 * (i % 2) - 1) * s) % Z * MEM + i for s in SLOTS] for i in range(MEM)]


def send(x, perm):
    return lax.ppermute(x, "mem", perm)


def stack(*blocks):
    return jnp.concatenate(blocks, axis=0)


def after(x, *done):
    return lax.optimization_barrier((x, *done))[0]


def ladder_partial(own, ready, multiply):
    rows = own.shape[0]
    a1 = send(own, RING)
    b1 = send(own, RING_SIBLING)
    q1 = send(own, RING_NEIGHBOUR)
    b0 = send(own, SIBLING)
    x0 = send(own, NEIGHBOUR)

    a1 = after(a1, ready)
    a2 = send(a1, RING)
    b1 = after(b1, a1, b0)
    b2 = send(b1, RING)
    r1 = send(b1, NEIGHBOUR)
    q1 = after(q1, b1)
    q2 = send(q1, RING)
    a2 = after(a2, q1)
    a3 = send(a2, RING)
    b2 = after(b2, a2)
    b3 = send(b2, RING)
    x0 = after(x0, b2)
    bx = send(x0, SIBLING)
    r2 = send(b2, NEIGHBOUR)
    q2 = after(q2, x0)
    q3 = send(q2, RING)
    a3 = after(a3, q2, bx)
    a4 = send(a3, RING)
    r1 = after(r1, a3)
    near = stack(b1, a1, r1, q1)
    c1 = send(near, SIBLING)
    a3 = after(a3, near)
    b3 = after(b3, a3)
    r3 = send(b3, NEIGHBOUR)
    q3 = after(q3, b3, c1)
    q4 = send(q3, RING)
    r2 = after(r2, q3)
    middle = stack(b2, a2, r2, q2)
    c2 = send(middle, SIBLING)
    product = multiply(stack(after(own, middle), b0, x0, bx, a1, b1, q1, r1, c1))
    partial = jnp.pad(product, ((0, 20 * rows), (0, 0)))
    r3 = after(r3, partial)
    third = stack(b3, a3, r3, q3)
    c3 = send(third, SIBLING)
    product = multiply(stack(after(a2, third), b2, q2, r2, c2))
    partial = lax.dynamic_update_slice(partial, product, (12 * rows, 0))
    a4 = after(a4, partial)
    q4 = after(q4, a4)
    fourth = stack(a4, q4)
    c4 = send(fourth, SIBLING)
    product = multiply(stack(after(a3, fourth), b3, q3, r3, c3))
    partial = lax.dynamic_update_slice(partial, product, (20 * rows, 0))
    c4 = after(c4, partial)
    product = multiply(stack(a4, c4[:rows], q4, c4[rows:]))
    return lax.dynamic_update_slice(partial, product, (28 * rows, 0))


def mask_kernel(cd_pairs, block_irrep, ab_blocks, scale):
    target = block_irrep[ab_blocks[0, 0]] ^ block_irrep[ab_blocks[1, 0]]
    symmetry = block_irrep[cd_pairs[0, 0]] ^ block_irrep[cd_pairs[0, 1]]
    scale[...] = jnp.full(scale.shape, jnp.where(symmetry == target, 32.0, 0.0), jnp.float32)


def local(
    contracted_amplitudes,
    ladder_integrals,
    cd_pairs,
    block_irrep,
    ab_blocks,
    amps_ab,
    dressing,
    occ_energy,
    virt_energy,
    pair_occ,
):
    col_count = ladder_integrals.shape[1]
    local_rows = amps_ab.shape[0]
    block_width = dressing.shape[1]
    pair_width = block_width * block_width
    block_total = dressing.shape[0]
    block_ids = jnp.arange(block_total, dtype=jnp.int32)
    out_onehot = (ab_blocks[:, :, None] == block_ids[None, None, :]).astype(jnp.int32)
    scale = pl.pallas_call(
        mask_kernel,
        out_shape=jax.ShapeDtypeStruct((1, 128), jnp.float32),
        in_specs=[pl.BlockSpec(memory_space=pltpu.SMEM)] * 3,
        out_specs=pl.BlockSpec(memory_space=pltpu.VMEM),
        compiler_params=pltpu.CompilerParams(vmem_limit_bytes=1 << 20),
    )(cd_pairs, block_irrep, ab_blocks.T)

    member = lax.axis_index("mem")
    x_lo = (member // 2) % 2
    core = member % 2

    def multiply(rows):
        rows = lax.optimization_barrier(rows)
        product = jnp.dot(rows, ladder_integrals, preferred_element_type=jnp.float32)
        return (product * scale[0, 0]).astype(jnp.float16)

    partial = ladder_partial(contracted_amplitudes, scale, multiply)
    partial = partial.reshape(Z, -1, col_count)
    partial = lax.all_to_all(partial, ("grp", "mem"), split_axis=0, concat_axis=0, axis_index_groups=OWNERS)
    summed = jnp.sum(partial.astype(jnp.float32), axis=0)
    summed = summed.reshape(2, 2, -1, col_count)
    summed = jnp.where(x_lo == 1, summed[::-1], summed)
    summed = jnp.where(core == 1, summed[:, ::-1], summed)
    summed = summed.reshape(MEM, local_rows, col_count).astype(jnp.float16)
    ladder = lax.all_to_all(summed, "mem", split_axis=0, concat_axis=0).astype(jnp.float32) * (1.0 / 32.0)

    out_pairs = ab_blocks.shape[0]
    left_select = out_onehot[:, 0, :].astype(jnp.float32)
    right_select = out_onehot[:, 1, :].astype(jnp.float32)
    dress_flat = dressing.reshape(block_total, pair_width).astype(jnp.float32)
    left_dress = jnp.dot(left_select, dress_flat, precision=lax.Precision.HIGHEST).reshape(
        out_pairs, block_width, block_width
    )
    right_dress = jnp.dot(right_select, dress_flat, precision=lax.Precision.HIGHEST).reshape(
        out_pairs, block_width, block_width
    )
    amp_blocks = amps_ab.astype(jnp.float32).reshape(
        local_rows, out_pairs, block_width, block_width
    )
    dressed = jnp.einsum("nac,pncb->pnab", left_dress, amp_blocks, precision=lax.Precision.HIGHEST)
    dressed = dressed + jnp.einsum(
        "nbc,pnac->pnab", right_dress, amp_blocks, precision=lax.Precision.HIGHEST
    )
    virt_blocks = virt_energy.reshape(block_total, block_width)
    left_energy = jnp.dot(left_select, virt_blocks, precision=lax.Precision.HIGHEST)
    right_energy = jnp.dot(right_select, virt_blocks, precision=lax.Precision.HIGHEST)
    occ_ids = jnp.arange(occ_energy.shape[0], dtype=jnp.int32)
    occ_onehot = (pair_occ[:, :, None] == occ_ids[None, None, :]).astype(jnp.float32)
    occ_pick = jnp.sum(occ_onehot * occ_energy[None, None, :], axis=-1)
    occ_sum = occ_pick[:, 0] + occ_pick[:, 1]
    denominator = (
        left_energy[None, :, :, None]
        + right_energy[None, :, None, :]
        - occ_sum[:, None, None, None]
    )
    width = out_pairs * pair_width
    dressed = dressed.reshape(local_rows, width)
    denominator = denominator.reshape(local_rows, width)
    ladder = ladder.transpose(1, 0, 2).reshape(local_rows, width)
    return (ladder + dressed) / denominator


def solution(mesh):
    return jax.shard_map(
        local,
        mesh=mesh,
        in_specs=(
            P("mem", "grp"),
            P("grp", "mem"),
            P("grp", None),
            P(),
            P(),
            P(("grp", "mem"), None),
            P(),
            P(),
            P(),
            P(("grp", "mem"), None),
        ),
        out_specs=P(("grp", "mem"), None),
        check_vma=False,
    )
```

```python
import jax
import jax.numpy as jnp
from jax import lax
from jax.experimental import pallas as pl
from jax.experimental.pallas import tpu as pltpu
from jax.sharding import PartitionSpec as P

Z = 8
MEM = 32


def pairs(target):
    return [(i, target(i)) for i in range(MEM)]


RING = pairs(lambda i: (i + 4) % MEM if i % 2 == 0 else (i - 4) % MEM)
NEIGHBOUR = pairs(lambda i: i ^ 2)
SIBLING = pairs(lambda i: i ^ 1)
RING_SIBLING = pairs(lambda i: (i - 3) % MEM if i % 2 == 0 else (i + 3) % MEM)
RING_NEIGHBOUR = pairs(lambda i: ((i + 4) % MEM if i % 2 == 0 else (i - 4) % MEM) ^ 2)


SLOTS = (0, 1, Z - 1, 2, Z - 2, 3, Z - 3, 4)
OWNERS = [[(i // 4 + (2 * (i % 2) - 1) * s) % Z * MEM + i for s in SLOTS] for i in range(MEM)]


def send(x, perm):
    return lax.ppermute(x, "mem", perm)


def stack(*blocks):
    return jnp.concatenate(blocks, axis=0)


def after(x, *done):
    return lax.optimization_barrier((x, *done))[0]


def ladder_partial(own, ready, multiply):
    rows = own.shape[0]
    a1 = send(own, RING)
    b1 = send(own, RING_SIBLING)
    q1 = send(own, RING_NEIGHBOUR)
    b0 = send(own, SIBLING)
    x0 = send(own, NEIGHBOUR)

    a1 = after(a1, ready)
    a2 = send(a1, RING)
    b1 = after(b1, a1, b0)
    b2 = send(b1, RING)
    r1 = send(b1, NEIGHBOUR)
    q1 = after(q1, b1)
    q2 = send(q1, RING)
    a2 = after(a2, q1)
    a3 = send(a2, RING)
    b2 = after(b2, a2)
    b3 = send(b2, RING)
    x0 = after(x0, b2)
    bx = send(x0, SIBLING)
    r2 = send(b2, NEIGHBOUR)
    q2 = after(q2, x0)
    q3 = send(q2, RING)
    a3 = after(a3, q2, bx)
    a4 = send(a3, RING)
    r1 = after(r1, a3)
    near = stack(b1, a1, r1, q1)
    c1 = send(near, SIBLING)
    a3 = after(a3, near)
    b3 = after(b3, a3)
    r3 = send(b3, NEIGHBOUR)
    q3 = after(q3, b3, c1)
    q4 = send(q3, RING)
    r2 = after(r2, q3)
    middle = stack(b2, a2, r2, q2)
    c2 = send(middle, SIBLING)
    product = multiply(stack(after(own, middle), b0, x0, bx, a1, b1, q1, r1, c1))
    partial = jnp.pad(product, ((0, 20 * rows), (0, 0)))
    r3 = after(r3, partial)
    third = stack(b3, a3, r3, q3)
    c3 = send(third, SIBLING)
    product = multiply(stack(after(a2, third), b2, q2, r2, c2))
    partial = lax.dynamic_update_slice(partial, product, (12 * rows, 0))
    a4 = after(a4, partial)
    q4 = after(q4, a4)
    fourth = stack(a4, q4)
    c4 = send(fourth, SIBLING)
    product = multiply(stack(after(a3, fourth), b3, q3, r3, c3))
    partial = lax.dynamic_update_slice(partial, product, (20 * rows, 0))
    c4 = after(c4, partial)
    product = multiply(stack(a4, c4[:rows], q4, c4[rows:]))
    return lax.dynamic_update_slice(partial, product, (28 * rows, 0))


def mask_kernel(cd_pairs, block_irrep, ab_blocks, scale):
    target = block_irrep[ab_blocks[0, 0]] ^ block_irrep[ab_blocks[1, 0]]
    symmetry = block_irrep[cd_pairs[0, 0]] ^ block_irrep[cd_pairs[0, 1]]
    scale[...] = jnp.full(scale.shape, jnp.where(symmetry == target, 32.0, 0.0), jnp.float32)


def local(
    contracted_amplitudes,
    ladder_integrals,
    cd_pairs,
    block_irrep,
    ab_blocks,
    amps_ab,
    dressing,
    occ_energy,
    virt_energy,
    pair_occ,
):
    col_count = ladder_integrals.shape[1]
    local_rows = amps_ab.shape[0]
    block_width = dressing.shape[1]
    pair_width = block_width * block_width
    block_total = dressing.shape[0]
    block_ids = jnp.arange(block_total, dtype=jnp.int32)
    out_onehot = (ab_blocks[:, :, None] == block_ids[None, None, :]).astype(jnp.int32)
    scale = pl.pallas_call(
        mask_kernel,
        out_shape=jax.ShapeDtypeStruct((1, 128), jnp.float32),
        in_specs=[pl.BlockSpec(memory_space=pltpu.SMEM)] * 3,
        out_specs=pl.BlockSpec(memory_space=pltpu.VMEM),
        compiler_params=pltpu.CompilerParams(vmem_limit_bytes=1 << 20),
    )(cd_pairs, block_irrep, ab_blocks.T)

    member = lax.axis_index("mem")
    x_lo = (member // 2) % 2
    core = member % 2

    def multiply(rows):
        rows = lax.optimization_barrier(rows)
        product = jnp.dot(rows, ladder_integrals, preferred_element_type=jnp.float32)
        return (product * scale[0, 0]).astype(jnp.float16)

    partial = ladder_partial(contracted_amplitudes, scale, multiply)
    partial = partial.reshape(Z, -1, col_count)
    partial = lax.all_to_all(partial, ("grp", "mem"), split_axis=0, concat_axis=0, axis_index_groups=OWNERS)
    summed = jnp.sum(partial.astype(jnp.float32), axis=0)
    summed = summed.reshape(2, 2, -1, col_count)
    summed = jnp.where(x_lo == 1, summed[::-1], summed)
    summed = jnp.where(core == 1, summed[:, ::-1], summed)
    summed = summed.reshape(MEM, local_rows, col_count).astype(jnp.float16)
    out_pairs = ab_blocks.shape[0]
    left_select = out_onehot[:, 0, :].astype(jnp.float32)
    right_select = out_onehot[:, 1, :].astype(jnp.float32)
    dress_flat = dressing.reshape(block_total, pair_width).astype(jnp.float32)
    left_dress = jnp.dot(left_select, dress_flat, precision=lax.Precision.HIGHEST).reshape(
        out_pairs, block_width, block_width
    )
    right_dress = jnp.dot(right_select, dress_flat, precision=lax.Precision.HIGHEST).reshape(
        out_pairs, block_width, block_width
    )
    amp_blocks = amps_ab.astype(jnp.float32).reshape(
        local_rows, out_pairs, block_width, block_width
    )
    dressed = jnp.einsum("nac,pncb->pnab", left_dress, amp_blocks, precision=lax.Precision.HIGHEST)
    dressed = dressed + jnp.einsum(
        "nbc,pnac->pnab", right_dress, amp_blocks, precision=lax.Precision.HIGHEST
    )
    virt_blocks = virt_energy.reshape(block_total, block_width)
    left_energy = jnp.dot(left_select, virt_blocks, precision=lax.Precision.HIGHEST)
    right_energy = jnp.dot(right_select, virt_blocks, precision=lax.Precision.HIGHEST)
    occ_ids = jnp.arange(occ_energy.shape[0], dtype=jnp.int32)
    occ_onehot = (pair_occ[:, :, None] == occ_ids[None, None, :]).astype(jnp.float32)
    occ_pick = jnp.sum(occ_onehot * occ_energy[None, None, :], axis=-1)
    occ_sum = occ_pick[:, 0] + occ_pick[:, 1]
    denominator = (
        left_energy[None, :, :, None]
        + right_energy[None, :, None, :]
        - occ_sum[:, None, None, None]
    )
    width = out_pairs * pair_width
    dressed = dressed.reshape(local_rows, width)
    denominator = denominator.reshape(local_rows, width)
    summed, dressed, denominator = lax.optimization_barrier((summed, dressed, denominator))
    ladder = lax.all_to_all(summed, "mem", split_axis=0, concat_axis=0).astype(jnp.float32) * (1.0 / 32.0)
    ladder = ladder.transpose(1, 0, 2).reshape(local_rows, width)
    return (ladder + dressed) / denominator


def solution(mesh):
    return jax.shard_map(
        local,
        mesh=mesh,
        in_specs=(
            P("mem", "grp"),
            P("grp", "mem"),
            P("grp", None),
            P(),
            P(),
            P(("grp", "mem"), None),
            P(),
            P(),
            P(),
            P(("grp", "mem"), None),
        ),
        out_specs=P(("grp", "mem"), None),
        check_vma=False,
    )
```
